128 devices in a mesh: area: 8 (over x, core), grp: 16 (over z, y).
Axes of the slice: x: 4, y: 4, z: 4, core: 2. Of those that a mesh axis runs over, the one named last changes fastest.
Arguments:
- spikes: int32 [10, 8, 512, 128], P(None, 'area', 'grp'), may hold values 0 or 1
- history: int32 [19, 8, 512, 128], P(None, 'area', 'grp'), may hold values 0 or 1
- intra_source: int32 [8, 16, 64], P('area', 'grp'), may hold values from 0 to 31
- intra_target: int32 [8, 16, 64], P('area', 'grp'), may hold values from 0 to 511, as said below
- intra_weight: float32 [8, 16, 64, 128, 128], P('area', 'grp'), may hold values from -1.25 to 1.25
- inter_area: int32 [8, 16, 48, 1], P('area', 'grp'), may hold values from 0 to 7; in each aligned block of 48 rows (0 to 47, 48 to 95, ..., all dimensions but the last counted through in order) at most 12 rows name the same one
- inter_source: int32 [8, 16, 48], P('area', 'grp'), may hold values from 0 to 31
- inter_block: int32 [8, 16, 48], P('area', 'grp'), may hold values from 0 to 511
- inter_delay: int32 [8, 16, 48], P('area', 'grp'), may hold values from 0 to 9
- inter_weight: float32 [8, 16, 48, 128, 128], P('area', 'grp'), may hold values from -1.25 to 1.25
- voltage_init: float32 [8, 512, 128], P('area', 'grp'), may hold values from -6 to 6
- synapse_init: float32 [8, 512, 128], P('area', 'grp'), may hold values from -6 to 6
- membrane_rate: float32 [8, 512, 128], P('area', 'grp'), may hold values from 0.05 to 0.5
- synapse_decay: float32 [8, 512, 128], P('area', 'grp'), may hold values from 0.4 to 0.9
Outputs:
- voltage: float32 [8, 512, 128], P('area', 'grp')
- synapse: float32 [8, 512, 128], P('area', 'grp')
The draws below stay inside these ranges and needn't reach their ends.
Inputs may be any that keep to these rules, and one draw needn't show every extreme that they name: `inter_area`: among the 48 tiles of one device no area is named more than 12 times, and some device names one area exactly 12 times. Among the 64 tiles of one device no value of intra_target // 32 occurs more than 8 times, and in every device one value occurs exactly 8 times.
All inputs are finite; a program needn't handle non-finite values. No bound on the sum of `spikes` or of `history` on one device may be relied on, other than what follows from the above.
Results may differ from the reference program's by a relative error of at most 0.0003.
Values sent between devices are 32-bit elements; how exact they have to be, the bound alone decides.
No kernel may reach another device: no remote copies, remote signals or barrier semaphores. Data moves between devices by JAX's collectives and lax.ppermute only.
A program may use at most 64 MiB of HBM per device.

```python
import math
import jax
import jax.numpy as jnp
import numpy as np
from jax import lax

B = 128
STEPS = 10
NBD = 32
KI = 64
KX = 48
NBA = 512
CAP = 12
ICAP = 8
N_AREA = 8
N_GRP = 16


def draw_intra_target(key, part):
    key = jax.random.fold_in(key, 11)
    first_key, sorting_key, shuffle_key, block_key = jax.random.split(key, 4)
    devices = N_AREA * N_GRP
    slot_total = N_GRP * ICAP
    slot_group = jnp.arange(slot_total, dtype=jnp.int32) // ICAP
    favoured = jax.random.randint(first_key, (devices,), 0, N_GRP, dtype=jnp.int32)
    ordering_indices = jax.vmap(lambda k: jax.random.permutation(k, slot_total))(jax.random.split(sorting_key, devices)).astype(jnp.int32)
    score = (slot_group[None, :] != favoured[:, None]).astype(jnp.int32) * slot_total + ordering_indices
    ranked = jnp.argsort(score, axis=1, stable=True).astype(jnp.int32)
    chosen = jnp.take_along_axis(jnp.broadcast_to(slot_group[None, :], (devices, slot_total)), ranked[:, :KI], axis=1)
    mixing = jax.vmap(lambda k: jax.random.permutation(k, KI))(jax.random.split(shuffle_key, devices)).astype(jnp.int32)
    chosen = jnp.take_along_axis(chosen, mixing, axis=1)
    blocks = jax.random.randint(block_key, (devices, KI), 0, NBD, dtype=jnp.int32)
    return (chosen * NBD + blocks).reshape(N_AREA, N_GRP, KI).astype(jnp.int32)


def plant(drawn, stream_key, least, largest):
    dims = drawn.shape
    place = [jax.random.randint(jax.random.fold_in(stream_key, axis), (), 0, dims[axis]) for axis in range(len(dims))]
    drawn = drawn.at[tuple(place)].set(least)
    longest = dims.index(max(dims))
    place[longest] = (place[longest] + 1) % dims[longest]
    return drawn.at[tuple(place)].set(largest)


def block_levels(key, dims, shards, smallest, largest):
    loudness, own = 1.0, jax.random.fold_in(key, 6)
    for dim, blocks in shards:
        steps = jnp.exp(jax.random.uniform(jax.random.fold_in(own, dim), (blocks,), jnp.float32, smallest / len(shards), largest / len(shards)))
        loudness = loudness * jnp.repeat(steps, dims[dim] // blocks).reshape([-1 if axis == dim else 1 for axis in range(len(dims))])
    return loudness


def shared_out(key, own, number, rows, amount, top, bound, slope):
    order = jax.random.permutation(key, amount)
    heavy_load, ordinary = load_shares(amount, rows * top, bound, slope, True), load_shares(amount, rows * top, bound, slope, False)
    places = jnp.arange(amount)

    def named(lengths, rotation):
        used = int((lengths > 0).sum())
        fixed = max(1, used // 4)
        shifted = fixed + (places - fixed + rotation * (used - fixed)) % max(1, amount - fixed)
        return jnp.zeros((amount,), jnp.int32).at[order[jnp.where(places < fixed, places, shifted)]].set(jnp.asarray(lengths, jnp.int32))

    lengths = jnp.where(number % 4 == 0, named(heavy_load, number // 4), named(ordinary, number - number // 4 - 1))
    mixed = jax.random.permutation(jax.random.fold_in(own, 3), amount)
    giver, sink = mixed[0:amount // 2 * 2:2], mixed[1:amount // 2 * 2:2]
    margin = jnp.minimum(lengths[giver] - 1, bound - lengths[sink]) // 2
    margin = jnp.where((giver == order[0]) | (sink == order[0]) | (lengths[sink] == 0), 0, jnp.maximum(margin, 0))
    shifted = jax.random.randint(jax.random.fold_in(own, 4), (amount // 2,), 0, 1 << 20) % (margin + 1)
    lengths = lengths.at[giver].add(-shifted).at[sink].add(shifted)
    items = jnp.searchsorted(jnp.cumsum(lengths), jnp.arange(rows * top), side="right").astype(jnp.int32)
    table = items.reshape(top, rows).T
    table = table[jax.random.permutation(jax.random.fold_in(own, 1), rows)]
    rotation = jax.random.randint(jax.random.fold_in(own, 2), (rows, 1), 0, top)
    return jnp.take_along_axis(table, (jnp.arange(top)[None, :] + rotation) % top, axis=1)


def load_shares(amount, total, limit, lean, full):
    portions = [(1 << 20) // math.isqrt(rank ** lean) + 1 for rank in range(1, amount + 1)]
    largest = limit if full else min(limit, max(-(-total // amount), total * portions[0] // sum(portions)))
    least = 1 if total - largest >= amount - 1 else 0
    counts, rest = [largest] + [least] * (amount - 1), total - largest - least * (amount - 1)
    while rest > 0:
        free = [i for i in range(1, amount) if counts[i] < largest] or [i for i in range(1, amount) if counts[i] < limit]
        pool, budget = sum([portions[i] for i in free]), rest
        for i in free:
            addition = min(limit - counts[i], max(1, budget * portions[i] // pool), rest)
            counts[i] = counts[i] + addition
            rest = rest - addition
    return np.array(counts)


def noise(key, shape, width, reach, pieces=(), held_as=jnp.bfloat16):
    result = jax.random.normal(key, shape, jnp.float32) * width
    if len(pieces) > 0:
        result = block_levels(key, shape, pieces, -0.22, 0.18) * result
    return jnp.clip(result, min=-reach, max=reach).astype(held_as)


def setup_inputs(seed: int = 0) -> dict:
    streams_of = jax.random.split(jax.random.key(seed), 15)
    spikes = plant((jax.random.randint(streams_of[0], (STEPS, N_AREA, NBA, B), 0, 10) < 1).astype(jnp.int32), jax.random.fold_in(streams_of[0], 1), 0, 1)
    history = plant((jax.random.randint(streams_of[1], (2 * STEPS - 1, N_AREA, NBA, B), 0, 10) < 1).astype(jnp.int32), jax.random.fold_in(streams_of[1], 1), 0, 1)
    intra_source = plant(jax.random.randint(streams_of[2], (N_AREA, N_GRP, KI), 0, NBD), jax.random.fold_in(streams_of[2], 1), 0, NBD - 1).astype(jnp.int32)
    intra_target = draw_intra_target(jax.random.fold_in(streams_of[14], 71), 0)
    intra_weight = noise(streams_of[4], (N_AREA, N_GRP, KI, B, B), (KI * B // (10 * NBD)) ** -0.5, 1.25, ((0, 8), (1, 16)), jnp.float32)
    inter_area_keys = jax.random.split(jax.random.fold_in(streams_of[5], 1), N_AREA * N_GRP * KX // KX)
    inter_area_turns = jax.random.permutation(jax.random.fold_in(streams_of[5], 3), N_AREA * N_GRP * KX // KX)
    inter_area = jax.vmap(lambda own, number: shared_out(jax.random.fold_in(streams_of[5], 2), own, number, KX, N_AREA, 1, CAP, 2))(inter_area_keys, inter_area_turns).reshape((N_AREA, N_GRP, KX, 1))
    inter_source = plant(jax.random.randint(streams_of[6], (N_AREA, N_GRP, KX), 0, NBD), jax.random.fold_in(streams_of[6], 1), 0, NBD - 1).astype(jnp.int32)
    inter_block = plant(jax.random.randint(streams_of[7], (N_AREA, N_GRP, KX), 0, NBA), jax.random.fold_in(streams_of[7], 1), 0, NBA - 1).astype(jnp.int32)
    inter_delay = plant(jax.random.randint(streams_of[8], (N_AREA, N_GRP, KX), 0, STEPS), jax.random.fold_in(streams_of[8], 1), 0, STEPS - 1).astype(jnp.int32)
    inter_weight = noise(streams_of[9], (N_AREA, N_GRP, KX, B, B), (KX * B // (10 * NBD)) ** -0.5, 1.25, ((0, 8), (1, 16)), jnp.float32)
    voltage_init = noise(streams_of[10], (N_AREA, NBA, B), 1.0, 6.0, ((0, 8), (1, 16)), jnp.float32)
    synapse_init = noise(streams_of[11], (N_AREA, NBA, B), 1.0, 6.0, ((0, 8), (1, 16)), jnp.float32)
    membrane_rate = jnp.clip(jnp.exp(math.log(0.5) - 2.3025851 * jax.random.uniform(streams_of[12], (N_AREA, NBA, B), jnp.float32) ** block_levels(streams_of[12], (N_AREA, NBA, B), ((0, 8), (1, 16)), -0.2, 0.2)), 0.05, 0.5)
    synapse_decay = jnp.clip(0.4 + 0.49999997 * jax.random.uniform(streams_of[13], (N_AREA, NBA, B), jnp.float32) ** block_levels(streams_of[13], (N_AREA, NBA, B), ((0, 8), (1, 16)), -0.2, 0.2), 0.4, 0.9)
    return {"spikes": spikes, "history": history, "intra_source": intra_source, "intra_target": intra_target, "intra_weight": intra_weight, "inter_area": inter_area, "inter_source": inter_source, "inter_block": inter_block, "inter_delay": inter_delay, "inter_weight": inter_weight, "voltage_init": voltage_init, "synapse_init": synapse_init, "membrane_rate": membrane_rate, "synapse_decay": synapse_decay}


RESET_LEVEL = -1.0


def reference(spikes, history, intra_source, intra_target, intra_weight, inter_area, inter_source, inter_block, inter_delay, inter_weight, voltage_init, synapse_init, membrane_rate, synapse_decay):
    peak_value = lax.Precision.HIGHEST
    area_blocks = NBD * N_GRP
    offsets = (jnp.arange(N_GRP, dtype=jnp.int32) * NBD)[:, None]
    block_ids = jnp.arange(area_blocks, dtype=jnp.int32)
    step_ids = jnp.arange(STEPS, dtype=jnp.int32)

    def intra_area(packed):
        area_spikes, source_blocks, target_blocks, tile_weights = packed
        spike_rows = area_spikes[:, (source_blocks + offsets).reshape(-1)].astype(jnp.float32)
        tile_contributions = jnp.einsum("tkn,knm->tkm", spike_rows, tile_weights.reshape(-1, B, B), precision=peak_value)
        picking_mask = (target_blocks.reshape(-1)[None, :] == block_ids[:, None]).astype(jnp.float32)
        return jnp.einsum("vg,lga->lva", picking_mask, tile_contributions, precision=peak_value)

    intra_current = lax.map(intra_area, (jnp.moveaxis(spikes, 1, 0), intra_source, intra_target, intra_weight))

    def inter_source_area(accumulated, packed):
        area_history, destination_areas, source_blocks, target_blocks, tile_delays, tile_weights = packed
        destination_areas = destination_areas.reshape(-1)
        target_blocks = target_blocks.reshape(-1)
        tile_delays = tile_delays.reshape(-1)
        source_blocks = (source_blocks + offsets).reshape(-1)
        time_rows = step_ids[None, :] + (STEPS - 1) - tile_delays[:, None]
        spike_rows = area_history[time_rows, source_blocks[:, None]].astype(jnp.float32)
        tile_contributions = jnp.einsum("ksn,knm->ksm", spike_rows, tile_weights.reshape(-1, B, B), precision=peak_value)
        accumulated = accumulated.at[destination_areas[:, None], step_ids[None, :], target_blocks[:, None]].add(tile_contributions)
        return accumulated, None

    starting_voltage = jnp.zeros((N_AREA, STEPS, area_blocks, B), jnp.float32)
    inter_current, _ = lax.scan(inter_source_area, starting_voltage, (jnp.moveaxis(history, 1, 0), inter_area, inter_source, inter_block, inter_delay, inter_weight))
    current = intra_current + inter_current
    voltage = voltage_init
    synapse = synapse_init
    for moment in range(STEPS):
        synapse = synapse_decay * synapse + current[:, moment]
        voltage = voltage + membrane_rate * (synapse - voltage)
        voltage = jnp.where(spikes[moment] == 1, RESET_LEVEL, voltage)
    return voltage, synapse
```

```python
import functools

import jax
import jax.numpy as jnp
from jax import lax
from jax.experimental import pallas as pl
from jax.experimental.pallas import tpu as pltpu
from jax.sharding import PartitionSpec as P

RESET_LEVEL = -1.0
STEPS = 10
ROOM = 12
SLOTS = 16
MIB = 1 << 20
FLAG = 127
COUNT = 126

SMEM = pl.BlockSpec(memory_space=pltpu.SMEM)
VMEM = pl.BlockSpec(memory_space=pltpu.VMEM)
ANY = pl.BlockSpec(memory_space=pl.ANY)


def product(rows, weight):
    high = weight.astype(jnp.bfloat16)
    low = (weight - high.astype(jnp.float32)).astype(jnp.bfloat16)
    rows = rows.astype(jnp.float32).astype(jnp.bfloat16)
    return jnp.dot(rows, high, preferred_element_type=jnp.float32) + jnp.dot(
        rows, low, preferred_element_type=jnp.float32
    )


def start_chunks(weight, buffer, sems, chunk):
    copies = []
    for c in range(buffer.shape[0] // chunk):
        part = pl.ds(c * chunk, chunk)
        copy = pltpu.make_async_copy(weight.at[0, 0, part], buffer.at[part], sems.at[c])
        copy.start()
        copies.append(copy)
    return copies


def lanes_of(shape):
    return (
        lax.broadcasted_iota(jnp.int32, shape, 0),
        lax.broadcasted_iota(jnp.int32, shape, 1),
    )


def inter_kernel(blocks, chunk, area, source, block, delay, history, weight, out, buffer, sems, place, count):
    tiles = buffer.shape[0]
    copies = start_chunks(weight, buffer, sems, chunk)
    out[...] = jnp.zeros_like(out)
    for a in range(8):
        count[a] = 0
    row, lane = lanes_of((8, 128))
    labels = jnp.full((8, 128), -1, jnp.int32)
    for k in range(tiles):
        a = area[0, 0, k, 0]
        rank = count[a]
        count[a] = rank + 1
        place[k] = a * 128 + rank
        labels = jnp.where((row == a) & (lane == rank), block[0, 0, k], labels)
    labels = labels.astype(jnp.float32)
    for a in range(8):
        out[pl.ds(a * 128 + STEPS * ROOM, 1), :] = labels[a : a + 1, :]
    for k in range(tiles):
        if k % chunk == 0:
            copies[k // chunk].wait()
        first = (STEPS - 1 - delay[0, 0, k]) * blocks + source[0, 0, k]
        rows = history[pl.ds(first, STEPS, stride=blocks), :]
        out[pl.ds(place[k], STEPS, stride=ROOM), :] = product(rows, buffer[k])


def intra_kernel(blocks, groups, chunk, source, target, spikes, weight, out, labels, table, count, buffer, sems, place):
    tiles = buffer.shape[0]
    copies = start_chunks(weight, buffer, sems, chunk)
    out[...] = jnp.zeros_like(out)
    span = out.shape[0] // groups
    row, lane = lanes_of((groups, 128))

    def clear(i, _):
        table[i] = -1
        return 0

    lax.fori_loop(0, groups * blocks, clear, 0, unroll=16)
    for h in range(groups):
        count[h] = 0
    marks = jnp.full((groups, 128), -1, jnp.int32)
    for k in range(tiles):
        b = target[0, 0, k]
        h = b // blocks
        known = table[b]
        slot = jnp.where(known < 0, count[h], known)
        table[b] = slot
        count[h] = jnp.maximum(count[h], slot + 1)
        place[k] = h * span + slot
        marks = jnp.where((row == h) & (lane == slot), b - h * blocks, marks)
    labels[...] = marks
    for k in range(tiles):
        if k % chunk == 0:
            copies[k // chunk].wait()
        rows = spikes[pl.ds(source[0, 0, k], STEPS, stride=blocks), :]
        spot = pl.ds(place[k], STEPS, stride=SLOTS)
        out[spot, :] = out[spot, :] + product(rows, buffer[k])


def merge_kernel(blocks, groups, arrived, labels, table_in, count_in, sums, out, names, table, count, state, sems):
    areas = arrived.shape[0] // 128
    copies = []
    for a in range(areas):
        copy = pltpu.make_async_copy(
            arrived.at[pl.ds(a * 128 + STEPS * ROOM, 1)], names.at[pl.ds(a, 1)], sems.at[a]
        )
        copy.start()
        copies.append(copy)
    span = out.shape[0] // groups
    row, lane = lanes_of((groups, 128))
    out[...] = sums[...]
    labels_out = labels[...]

    def copy_table(i, _):
        table[i] = table_in[i]
        return 0

    lax.fori_loop(0, groups * blocks, copy_table, 0, unroll=16)
    for h in range(groups):
        count[h] = count_in[h]
    for copy in copies:
        copy.wait()
    marks = labels_out
    state[0] = 0
    for a in range(areas):

        def body(r, carry, a=a):
            marks, going = carry
            b = names[a, r].astype(jnp.int32)
            live = b >= 0
            b = jnp.maximum(b, 0)
            h = b // blocks
            known = table[b]
            slot = jnp.where(known < 0, count[h], known)
            fits = live & (slot < SLOTS)

            @pl.when(fits)
            def _():
                table[b] = slot
                count[h] = jnp.maximum(count[h], slot + 1)
                spot = pl.ds(h * span + slot, STEPS, stride=SLOTS)
                out[spot, :] = out[spot, :] + arrived[pl.ds(a * 128 + r, STEPS, stride=ROOM), :]

            @pl.when(live & (slot >= SLOTS))
            def _():
                state[0] = 1

            marks = jnp.where((row == h) & (lane == slot) & fits, b - h * blocks, marks)
            return marks, going

        marks, _ = lax.fori_loop(0, ROOM, body, (marks, 0))
    for h in range(groups):
        marks = jnp.where((row == h) & (lane == COUNT), count[h], marks)
    marks = jnp.where(lane == FLAG, state[0], marks).astype(jnp.float32)
    for h in range(groups):
        out[pl.ds(h * span + STEPS * SLOTS, 1), :] = marks[h : h + 1, :]


def advance(voltage, synapse, current, spiked, rate, decay):
    synapse = decay * synapse + current
    voltage = voltage + rate * (synapse - voltage)
    return jnp.where(spiked == 1, RESET_LEVEL, voltage), synapse


def advance_kernel(blocks, groups, arrived, spikes, voltage, synapse, rate, decay, v_out, s_out, flag, names, total, sems):
    span = arrived.shape[0] // groups
    copies = []
    for h in range(groups):
        copy = pltpu.make_async_copy(
            arrived.at[pl.ds(h * span + STEPS * SLOTS, 1)], names.at[pl.ds(h, 1)], sems.at[h]
        )
        copy.start()
        copies.append(copy)
    total[...] = jnp.zeros_like(total)
    for copy in copies:
        copy.wait()
    raised = jnp.int32(0)
    for h in range(groups):
        raised = jnp.maximum(raised, names[h, FLAG].astype(jnp.int32))

        def body(j, _, h=h):
            spot = pl.ds(names[h, j].astype(jnp.int32), STEPS, stride=blocks)
            total[spot, :] = total[spot, :] + arrived[pl.ds(h * span + j, STEPS, stride=SLOTS), :]
            return 0

        lax.fori_loop(0, names[h, COUNT].astype(jnp.int32), body, 0)
    flag[0] = raised
    v, s = voltage[0], synapse[0]
    for t in range(STEPS):
        part = pl.ds(t * blocks, blocks)
        v, s = advance(v, s, total[part, :], spikes[part, :], rate[0], decay[0])
    v_out[0] = v
    s_out[0] = s


def dense_path(blocks, groups, arrived, intra_source, intra_target, intra_weight, spikes, voltage, synapse, rate, decay):
    exact = lax.Precision.HIGHEST
    ids = jnp.arange(groups * blocks, dtype=jnp.int32)
    areas = arrived.shape[0] // 128
    messages = arrived.reshape(areas, 128, 128)
    names = messages[:, STEPS * ROOM, :ROOM].reshape(-1).astype(jnp.int32)
    delayed = messages[:, : STEPS * ROOM].reshape(areas, STEPS, ROOM, 128)
    delayed = delayed.transpose(0, 2, 1, 3).reshape(areas * ROOM, STEPS * 128)
    rows = spikes.reshape(STEPS, blocks, 128)[:, intra_source.reshape(-1)].astype(jnp.float32)
    own = jnp.einsum("tkn,knm->ktm", rows, intra_weight[0, 0], precision=exact)
    own = own.reshape(-1, STEPS * 128)
    pick = (ids[:, None] == intra_target.reshape(-1)[None, :]).astype(jnp.float32)
    put = (ids[:, None] == names[None, :]).astype(jnp.float32)
    sums = jnp.dot(pick, own, precision=exact) + jnp.dot(put, delayed, precision=exact)
    parts = lax.all_to_all(
        sums.reshape(groups, blocks, STEPS * 128), "grp", split_axis=0, concat_axis=0, tiled=True
    )
    total = parts.sum(0).reshape(blocks, STEPS, 128)
    v, s = voltage[0], synapse[0]
    steps = spikes.reshape(STEPS, blocks, 128)
    for t in range(STEPS):
        v, s = advance(v, s, total[:, t], steps[t], rate[0], decay[0])
    return v[None], s[None]


def shards(
    spikes,
    history,
    intra_source,
    intra_target,
    intra_weight,
    inter_area,
    inter_source,
    inter_block,
    inter_delay,
    inter_weight,
    voltage_init,
    synapse_init,
    membrane_rate,
    synapse_decay,
):
    blocks, width = spikes.shape[2:]
    groups, areas = lax.axis_size("grp"), lax.axis_size("area")
    inter_tiles, intra_tiles = inter_weight.shape[2], intra_weight.shape[2]
    spikes = spikes.reshape(STEPS * blocks, width)
    history = history.reshape(-1, width)
    span = STEPS * SLOTS + 8
    chunk = 8
    params = pltpu.CompilerParams(vmem_limit_bytes=32 * MIB)

    outgoing = pl.pallas_call(
        functools.partial(inter_kernel, blocks, chunk),
        out_shape=jax.ShapeDtypeStruct((areas * 128, width), jnp.float32),
        in_specs=[SMEM] * 4 + [VMEM, ANY],
        out_specs=VMEM,
        scratch_shapes=[
            pltpu.VMEM((inter_tiles, width, width), jnp.float32),
            pltpu.SemaphoreType.DMA((inter_tiles // chunk,)),
            pltpu.SMEM((inter_tiles,), jnp.int32),
            pltpu.SMEM((areas,), jnp.int32),
        ],
        compiler_params=params,
        name="inter",
    )(inter_area, inter_source, inter_block, inter_delay, history, inter_weight)
    arrived = lax.all_to_all(
        outgoing.reshape(areas, 128, width), "area", split_axis=0, concat_axis=0, tiled=True
    ).reshape(areas * 128, width)

    sums, labels, table, count = pl.pallas_call(
        functools.partial(intra_kernel, blocks, groups, chunk),
        out_shape=(
            jax.ShapeDtypeStruct((groups * span, width), jnp.float32),
            jax.ShapeDtypeStruct((groups, 128), jnp.int32),
            jax.ShapeDtypeStruct((groups * blocks,), jnp.int32),
            jax.ShapeDtypeStruct((groups,), jnp.int32),
        ),
        in_specs=[SMEM, SMEM, VMEM, ANY],
        out_specs=(VMEM, VMEM, SMEM, SMEM),
        scratch_shapes=[
            pltpu.VMEM((intra_tiles, width, width), jnp.float32),
            pltpu.SemaphoreType.DMA((intra_tiles // chunk,)),
            pltpu.SMEM((intra_tiles,), jnp.int32),
        ],
        compiler_params=params,
        cost_estimate=pl.CostEstimate(flops=10**9, bytes_accessed=10**7, transcendentals=0),
        name="intra",
    )(intra_source, intra_target, spikes, intra_weight)

    message = pl.pallas_call(
        functools.partial(merge_kernel, blocks, groups),
        out_shape=jax.ShapeDtypeStruct((groups * span, width), jnp.float32),
        in_specs=[VMEM, VMEM, SMEM, SMEM, VMEM],
        out_specs=VMEM,
        scratch_shapes=[
            pltpu.SMEM((areas, 128), jnp.float32),
            pltpu.SMEM((groups * blocks,), jnp.int32),
            pltpu.SMEM((groups,), jnp.int32),
            pltpu.SMEM((1,), jnp.int32),
            pltpu.SemaphoreType.DMA((areas,)),
        ],
        compiler_params=params,
        name="merge",
    )(arrived, labels, table, count, sums)
    parts = lax.all_to_all(
        message.reshape(groups, span, width), "grp", split_axis=0, concat_axis=0, tiled=True
    ).reshape(groups * span, width)

    state = (voltage_init, synapse_init, membrane_rate, synapse_decay)
    voltage, synapse, flag = pl.pallas_call(
        functools.partial(advance_kernel, blocks, groups),
        out_shape=(
            jax.ShapeDtypeStruct(voltage_init.shape, jnp.float32),
            jax.ShapeDtypeStruct(voltage_init.shape, jnp.float32),
            jax.ShapeDtypeStruct((1,), jnp.int32),
        ),
        in_specs=[VMEM] * 6,
        out_specs=(VMEM, VMEM, SMEM),
        scratch_shapes=[
            pltpu.SMEM((groups, 128), jnp.float32),
            pltpu.VMEM((STEPS * blocks, width), jnp.float32),
            pltpu.SemaphoreType.DMA((groups,)),
        ],
        compiler_params=params,
        name="advance",
    )(parts, spikes, *state)

    def whole(_):
        return dense_path(
            blocks, groups, arrived, intra_source, intra_target, intra_weight, spikes, *state
        )

    return lax.cond(flag[0] > 0, whole, lambda done: done, (voltage, synapse))


def solution(mesh):
    in_specs = (
        P(None, "area", "grp", None),
        P(None, "area", "grp", None),
        P("area", "grp", None),
        P("area", "grp", None),
        P("area", "grp", None, None, None),
        P("area", "grp", None, None),
        P("area", "grp", None),
        P("area", "grp", None),
        P("area", "grp", None),
        P("area", "grp", None, None, None),
        P("area", "grp", None),
        P("area", "grp", None),
        P("area", "grp", None),
        P("area", "grp", None),
    )
    out_specs = (P("area", "grp", None), P("area", "grp", None))
    return jax.shard_map(shards, mesh=mesh, in_specs=in_specs, out_specs=out_specs, check_vma=False)
```

```python
import functools

import jax
import jax.numpy as jnp
from jax import lax
from jax.experimental import pallas as pl
from jax.experimental.pallas import tpu as pltpu
from jax.sharding import PartitionSpec as P

RESET_LEVEL = -1.0
STEPS = 10
ROOM = 12
SPAN = 128
CHUNK = 8
MIB = 1 << 20

SMEM = pl.BlockSpec(memory_space=pltpu.SMEM)
VMEM = pl.BlockSpec(memory_space=pltpu.VMEM)
ANY = pl.BlockSpec(memory_space=pl.ANY)


def started(copies):
    copies = list(copies)
    for copy in copies:
        copy.start()
    return copies


def prepare_kernel(blocks, groups, spikes_in, decay_in, rate_in, out, spikes, tile, sems, out_sems):
    copies = started(
        [
            pltpu.make_async_copy(spikes_in, spikes, sems.at[0]),
            pltpu.make_async_copy(decay_in.at[0], tile.at[pl.ds(0, blocks)], sems.at[1]),
            pltpu.make_async_copy(rate_in.at[0], tile.at[pl.ds(blocks, blocks)], sems.at[2]),
        ]
    )
    copies[0].wait()
    last = jnp.full((blocks, 128), -1.0, jnp.float32)
    for t in range(STEPS):
        last = jnp.where(spikes[pl.ds(t * blocks, blocks), :] == 1, float(t), last)
    tile[pl.ds(2 * blocks, blocks), :] = last
    copies[1].wait()
    copies[2].wait()
    rows = 3 * blocks
    for copy in started(
        pltpu.make_async_copy(tile, out.at[pl.ds(h * rows, rows)], out_sems.at[h]) for h in range(groups)
    ):
        copy.wait()


def product(rows, weight):
    high = weight.astype(jnp.bfloat16)
    low = (weight - high.astype(jnp.float32)).astype(jnp.bfloat16)
    rows = rows.astype(jnp.float32).astype(jnp.bfloat16)
    return jnp.dot(rows, high, preferred_element_type=jnp.float32) + jnp.dot(
        rows, low, preferred_element_type=jnp.float32
    )


def tiles_kernel(
    blocks,
    areas,
    span,
    area,
    inter_source,
    inter_block,
    delay,
    intra_source,
    intra_target,
    history_in,
    spikes_in,
    inter_in,
    intra_in,
    out,
    total,
    history,
    spikes,
    inter,
    intra,
    inter_sems,
    intra_sems,
    row_sems,
    place,
    count,
):
    row_copies = started(
        [
            pltpu.make_async_copy(history_in, history, row_sems.at[0]),
            pltpu.make_async_copy(spikes_in, spikes, row_sems.at[1]),
        ]
    )

    def chunks(source, target, sems):
        return started(
            pltpu.make_async_copy(
                source.at[0, 0, pl.ds(c * CHUNK, CHUNK)], target.at[pl.ds(c * CHUNK, CHUNK)], sems.at[c]
            )
            for c in range(target.shape[0] // CHUNK)
        )

    inter_copies = chunks(inter_in, inter, inter_sems)
    intra_copies = chunks(intra_in, intra, intra_sems)
    out[...] = jnp.zeros_like(out)
    for a in range(areas):
        count[a] = 0
    row = lax.broadcasted_iota(jnp.int32, (areas, 128), 0)
    lane = lax.broadcasted_iota(jnp.int32, (areas, 128), 1)
    names = jnp.full((areas, 128), -1, jnp.int32)
    for k in range(inter.shape[0]):
        a = area[0, 0, 0, k]
        rank = count[a]
        count[a] = rank + 1
        place[k] = a * SPAN + rank
        names = jnp.where((row == a) & (lane == rank), inter_block[0, 0, k], names)
    names = names.astype(jnp.float32)
    for a in range(areas):
        out[pl.ds(a * SPAN + STEPS * ROOM, 1), :] = names[a : a + 1, :]
    row_copies[0].wait()
    for k in range(inter.shape[0]):
        if k % CHUNK == 0:
            inter_copies[k // CHUNK].wait()
        first = (STEPS - 1 - delay[0, 0, k]) * blocks + inter_source[0, 0, k]
        rows = history[pl.ds(first, STEPS, stride=blocks), :]
        out[pl.ds(place[k], STEPS, stride=ROOM), :] = product(rows, inter[k])
    total[...] = jnp.zeros_like(total)
    row_copies[1].wait()
    for k in range(intra.shape[0]):
        if k % CHUNK == 0:
            intra_copies[k // CHUNK].wait()
        rows = spikes[pl.ds(intra_source[0, 0, k], STEPS, stride=blocks), :]
        spot = pl.ds(intra_target[0, 0, k], STEPS, stride=span)
        total[spot, :] = total[spot, :] + product(rows, intra[k])


def contracted(blocks, span, total, params, h):
    base = h * 3 * blocks
    decay = params[pl.ds(base, blocks), :]
    rate = params[pl.ds(base + blocks, blocks), :]
    last = params[pl.ds(base + 2 * blocks, blocks), :]
    synapse = jnp.zeros((blocks, 128), jnp.float32)
    voltage = synapse
    for t in range(STEPS):
        synapse = decay * synapse + total[pl.ds(t * span + h * blocks, blocks), :]
        voltage = voltage + rate * (synapse - voltage)
        voltage = jnp.where(last == float(t), 0.0, voltage)
    return synapse, voltage


def contract_kernel(blocks, groups, span, total, params, out):
    def body(h, _):
        h = pl.multiple_of(h, 1)
        synapse, voltage = contracted(blocks, span, total, params, h)
        out[pl.ds(h * 2 * blocks, blocks), :] = synapse
        out[pl.ds(h * 2 * blocks + blocks, blocks), :] = voltage
        return 0

    lax.fori_loop(0, groups, body, 0, unroll=4)


def merge_kernel(blocks, groups, areas, span, arrived, params, part, out, total, names, sems):
    copies = started(
        pltpu.make_async_copy(
            arrived.at[pl.ds(a * SPAN + STEPS * ROOM, 1)], names.at[pl.ds(a, 1)], sems.at[a]
        )
        for a in range(areas)
    )
    total[...] = jnp.zeros_like(total)
    for copy in copies:
        copy.wait()
    for a in range(areas):
        for r in range(ROOM):
            b = names[a, r].astype(jnp.int32)
            spot = pl.ds(jnp.where(b < 0, groups * blocks, b), STEPS, stride=span)
            total[spot, :] = total[spot, :] + arrived[pl.ds(a * SPAN + r, STEPS, stride=ROOM), :]

    def body(h, _):
        synapse, voltage = contracted(blocks, span, total, params, h)
        here = pl.ds(h * 2 * blocks, blocks)
        out[here, :] = part[here, :] + synapse
        here = pl.ds(h * 2 * blocks + blocks, blocks)
        out[here, :] = part[here, :] + voltage
        return 0

    lax.fori_loop(0, groups, body, 0, unroll=4)


def finish_kernel(blocks, groups, arrived, spikes, voltage_in, synapse_in, rate_in, decay_in, voltage_out, synapse_out):
    voltage, synapse, rate, decay = voltage_in[0], synapse_in[0], rate_in[0], decay_in[0]
    for t in range(STEPS):
        synapse = decay * synapse
        voltage = voltage + rate * (synapse - voltage)
        voltage = jnp.where(spikes[pl.ds(t * blocks, blocks), :] == 1, RESET_LEVEL, voltage)
    synapse_sum = arrived[pl.ds(0, blocks), :]
    voltage_sum = arrived[pl.ds(blocks, blocks), :]
    for h in range(1, groups):
        synapse_sum += arrived[pl.ds(h * 2 * blocks, blocks), :]
        voltage_sum += arrived[pl.ds(h * 2 * blocks + blocks, blocks), :]
    voltage_out[0] = voltage + voltage_sum
    synapse_out[0] = synapse + synapse_sum


def exchange(rows, axis, parts):
    width = rows.shape[1]
    rows = rows.reshape(parts, -1, width)
    return lax.all_to_all(rows, axis, split_axis=0, concat_axis=0, tiled=True).reshape(-1, width)


def shards(
    spikes,
    history,
    intra_source,
    intra_target,
    intra_weight,
    inter_area,
    inter_source,
    inter_block,
    inter_delay,
    inter_weight,
    voltage_init,
    synapse_init,
    membrane_rate,
    synapse_decay,
):
    blocks, width = spikes.shape[2:]
    groups, areas = lax.axis_size("grp"), lax.axis_size("area")
    inter_tiles, intra_tiles = inter_weight.shape[2], intra_weight.shape[2]
    spikes = spikes.reshape(STEPS * blocks, width)
    history = history.reshape(-1, width)
    span = groups * blocks + 8
    dma = pltpu.SemaphoreType.DMA

    def shape(rows):
        return jax.ShapeDtypeStruct((rows, width), jnp.float32)

    def params_of(limit):
        return pltpu.CompilerParams(vmem_limit_bytes=limit * MIB)

    def cost(us):
        return pl.CostEstimate(flops=us * 10**9, bytes_accessed=us * 3 * 10**6, transcendentals=0)

    own = pl.pallas_call(
        functools.partial(prepare_kernel, blocks, groups),
        out_shape=shape(groups * 3 * blocks),
        in_specs=[ANY] * 3,
        out_specs=ANY,
        scratch_shapes=[
            pltpu.VMEM(spikes.shape, jnp.int32),
            pltpu.VMEM((3 * blocks, width), jnp.float32),
            dma((3,)),
            dma((groups,)),
        ],
        compiler_params=params_of(56),
        cost_estimate=cost(1),
        name="prepare",
    )(spikes, synapse_decay, membrane_rate)
    params = exchange(own, "grp", groups)

    outgoing, total = pl.pallas_call(
        functools.partial(tiles_kernel, blocks, areas, span),
        out_shape=(shape(areas * SPAN), shape(STEPS * span)),
        in_specs=[SMEM] * 6 + [ANY] * 4,
        out_specs=(VMEM, VMEM),
        scratch_shapes=[
            pltpu.VMEM(history.shape, jnp.int32),
            pltpu.VMEM(spikes.shape, jnp.int32),
            pltpu.VMEM((inter_tiles, width, width), jnp.float32),
            pltpu.VMEM((intra_tiles, width, width), jnp.float32),
            dma((inter_tiles // CHUNK,)),
            dma((intra_tiles // CHUNK,)),
            dma((2,)),
            pltpu.SMEM((inter_tiles,), jnp.int32),
            pltpu.SMEM((areas,), jnp.int32),
        ],
        compiler_params=params_of(40),
        cost_estimate=cost(7),
        name="tiles",
    )(
        jnp.swapaxes(inter_area, 2, 3),
        inter_source,
        inter_block,
        inter_delay,
        intra_source,
        intra_target,
        history,
        spikes,
        inter_weight,
        intra_weight,
    )
    arrived = exchange(outgoing, "area", areas)

    part = pl.pallas_call(
        functools.partial(contract_kernel, blocks, groups, span),
        out_shape=shape(groups * 2 * blocks),
        in_specs=[VMEM] * 2,
        out_specs=VMEM,
        compiler_params=params_of(24),
        cost_estimate=cost(2),
        name="contract",
    )(total, params)

    message = pl.pallas_call(
        functools.partial(merge_kernel, blocks, groups, areas, span),
        out_shape=shape(groups * 2 * blocks),
        in_specs=[VMEM] * 3,
        out_specs=VMEM,
        scratch_shapes=[
            pltpu.VMEM((STEPS * span, width), jnp.float32),
            pltpu.SMEM((areas, 128), jnp.float32),
            dma((areas,)),
        ],
        compiler_params=params_of(24),
        cost_estimate=cost(2),
        name="merge",
    )(arrived, params, part)
    sums = exchange(message, "grp", groups)

    return pl.pallas_call(
        functools.partial(finish_kernel, blocks, groups),
        out_shape=(jax.ShapeDtypeStruct(voltage_init.shape, jnp.float32),) * 2,
        in_specs=[VMEM] * 6,
        out_specs=(VMEM, VMEM),
        compiler_params=params_of(24),
        cost_estimate=cost(1),
        name="finish",
    )(sums, spikes, voltage_init, synapse_init, membrane_rate, synapse_decay)


def solution(mesh):
    in_specs = (
        P(None, "area", "grp", None),
        P(None, "area", "grp", None),
        P("area", "grp", None),
        P("area", "grp", None),
        P("area", "grp", None, None, None),
        P("area", "grp", None, None),
        P("area", "grp", None),
        P("area", "grp", None),
        P("area", "grp", None),
        P("area", "grp", None, None, None),
        P("area", "grp", None),
        P("area", "grp", None),
        P("area", "grp", None),
        P("area", "grp", None),
    )
    out_specs = (P("area", "grp", None), P("area", "grp", None))
    return jax.shard_map(shards, mesh=mesh, in_specs=in_specs, out_specs=out_specs, check_vma=False)
```

```python
import functools

import jax
import jax.numpy as jnp
from jax import lax
from jax.experimental import pallas as pl
from jax.experimental.pallas import tpu as pltpu
from jax.sharding import PartitionSpec as P

RESET_LEVEL = -1.0
STEPS = 10
ROOM = 12
SPAN = 128
CHUNK = 16
LIMITS = (60, 4, 8)
MIB = 1 << 20

SMEM = pl.BlockSpec(memory_space=pltpu.SMEM)
VMEM = pl.BlockSpec(memory_space=pltpu.VMEM)
ANY = pl.BlockSpec(memory_space=pl.ANY)


def started(copies):
    copies = list(copies)
    for copy in copies:
        copy.start()
    return copies


def product(rows, weight):
    high = weight.astype(jnp.bfloat16)
    low = (weight - high.astype(jnp.float32)).astype(jnp.bfloat16)
    rows = rows.astype(jnp.float32).astype(jnp.bfloat16)
    both = jnp.concatenate([high, low], axis=0)
    return jnp.dot(jnp.concatenate([rows, rows], axis=1), both, preferred_element_type=jnp.float32)


def first_kernel(blocks, groups, areas, *refs):
    inputs, own, messages, rest = refs[:9], refs[9], refs[10:15], refs[15:]
    area, source, block, delay, spikes, decay, rate, history, weight = rest[:9]
    out, tile, sems, weight_sems, own_sems, out_sems, place, count = rest[9:]
    rows = 3 * blocks
    targets = (
        area,
        source,
        block,
        delay,
        spikes,
        tile.at[pl.ds(0, blocks)],
        tile.at[pl.ds(blocks, blocks)],
        history,
    )
    copies = started(
        pltpu.make_async_copy(inputs[i].at[0] if i in (5, 6) else inputs[i], target, sems.at[i])
        for i, target in enumerate(targets)
    )
    tiles = weight.shape[0]
    weight_copies = started(
        pltpu.make_async_copy(
            inputs[8].at[0, 0, pl.ds(c * CHUNK, CHUNK)], weight.at[pl.ds(c * CHUNK, CHUNK)], weight_sems.at[c]
        )
        for c in range(tiles // CHUNK)
    )
    out[...] = jnp.zeros_like(out)
    for a in range(areas):
        count[a] = 0
    for copy in copies[4:7]:
        copy.wait()
    last = jnp.full((blocks, 128), -1.0, jnp.float32)
    for t in range(STEPS):
        last = jnp.where(spikes[pl.ds(t * blocks, blocks), :] == 1, float(t), last)
    tile[pl.ds(2 * blocks, blocks), :] = last
    own_copies = started(
        pltpu.make_async_copy(tile, own.at[pl.ds(h * rows, rows)], own_sems.at[h]) for h in range(groups)
    )
    for copy in copies[:4]:
        copy.wait()
    me = lax.axis_index("area")
    row = lax.broadcasted_iota(jnp.int32, (areas, 128), 0)
    lane = lax.broadcasted_iota(jnp.int32, (areas, 128), 1)
    names = jnp.full((areas, 128), -1, jnp.int32)
    for k in range(tiles):
        a = area[0, 0, 0, k] ^ me
        rank = count[a]
        count[a] = rank + 1
        place[k] = a * SPAN + rank
        names = jnp.where((row == a) & (lane == rank), block[0, 0, k], names)
    names = names.astype(jnp.float32)
    for a in range(areas):
        out[pl.ds(a * SPAN + STEPS * ROOM, 1), :] = names[a : a + 1, :]
    copies[7].wait()
    for k in range(tiles):
        if k % CHUNK == 0:
            weight_copies[k // CHUNK].wait()
        first = (STEPS - 1 - delay[0, 0, k]) * blocks + source[0, 0, k]
        picked = history[pl.ds(first, STEPS, stride=blocks), :]
        out[pl.ds(place[k], STEPS, stride=ROOM), :] = product(picked, weight[k])
    out_copies = started(
        pltpu.make_async_copy(out.at[pl.ds(first * SPAN, message.shape[0])], message, out_sems.at[j])
        for j, (first, message) in enumerate(zip((0, 1, 2, 4, 6), messages))
    )
    for copy in own_copies + out_copies:
        copy.wait()


def clear_kernel(out):
    out[...] = jnp.zeros_like(out)


def intra_kernel(blocks, source, zeros, spikes, weight, out):
    tiles = weight.shape[2]
    for k in range(tiles):
        rows = spikes[pl.ds(source[0, 0, k], STEPS, stride=blocks), :]
        out[pl.ds(k, STEPS, stride=tiles), :] = product(rows, weight[0, 0, k])
    out[pl.ds(STEPS * tiles, 8), :] = zeros[...]


def contracted(blocks, span, total, params, h):
    base = h * 3 * blocks
    decay = params[pl.ds(base, blocks), :]
    rate = params[pl.ds(base + blocks, blocks), :]
    last = params[pl.ds(base + 2 * blocks, blocks), :]
    synapse = jnp.zeros((blocks, 128), jnp.float32)
    voltage = synapse
    for t in range(STEPS):
        synapse = decay * synapse + total[pl.ds(t * span + h * blocks, blocks), :]
        voltage = voltage + rate * (synapse - voltage)
        voltage = jnp.where(last == float(t), 0.0, voltage)
    return synapse, voltage


def merge_kernel(blocks, groups, areas, span, target, params, intra, *refs):
    arrived = refs[:areas]
    out, total, names, sems = refs[areas:]
    copies = started(
        pltpu.make_async_copy(arrived[a].at[pl.ds(STEPS * ROOM, 1)], names.at[pl.ds(a, 1)], sems.at[a])
        for a in range(areas)
    )
    total[...] = jnp.zeros_like(total)
    tiles = target.shape[2]
    for k in range(tiles):
        spot = pl.ds(target[0, 0, k], STEPS, stride=span)
        total[spot, :] = total[spot, :] + intra[pl.ds(k, STEPS, stride=tiles), :]
    for copy in copies:
        copy.wait()
    for a in range(areas):
        for r in range(ROOM):
            b = names[a, r].astype(jnp.int32)
            spot = pl.ds(jnp.where(b < 0, groups * blocks, b), STEPS, stride=span)
            total[spot, :] = total[spot, :] + arrived[a][pl.ds(r, STEPS, stride=ROOM), :]

    def body(h, _):
        synapse, voltage = contracted(blocks, span, total, params, h)
        out[pl.ds(h * 2 * blocks, blocks), :] = synapse
        out[pl.ds(h * 2 * blocks + blocks, blocks), :] = voltage
        return 0

    lax.fori_loop(0, groups, body, 0, unroll=4)


def finish_kernel(blocks, groups, arrived, spikes, voltage_in, synapse_in, rate_in, decay_in, voltage_out, synapse_out):
    voltage, synapse, rate, decay = voltage_in[0], synapse_in[0], rate_in[0], decay_in[0]
    for t in range(STEPS):
        synapse = decay * synapse
        voltage = voltage + rate * (synapse - voltage)
        voltage = jnp.where(spikes[pl.ds(t * blocks, blocks), :] == 1, RESET_LEVEL, voltage)
    synapse_sum = arrived[pl.ds(0, blocks), :]
    voltage_sum = arrived[pl.ds(blocks, blocks), :]
    for h in range(1, groups):
        synapse_sum += arrived[pl.ds(h * 2 * blocks, blocks), :]
        voltage_sum += arrived[pl.ds(h * 2 * blocks + blocks, blocks), :]
    voltage_out[0] = voltage + voltage_sum
    synapse_out[0] = synapse + synapse_sum


def exchange(rows, axis, parts):
    width = rows.shape[1]
    rows = rows.reshape(parts, -1, width)
    return lax.all_to_all(rows, axis, split_axis=0, concat_axis=0, tiled=True).reshape(-1, width)


def shards(
    spikes,
    history,
    intra_source,
    intra_target,
    intra_weight,
    inter_area,
    inter_source,
    inter_block,
    inter_delay,
    inter_weight,
    voltage_init,
    synapse_init,
    membrane_rate,
    synapse_decay,
):
    blocks, width = spikes.shape[2:]
    groups, areas = lax.axis_size("grp"), lax.axis_size("area")
    spikes = spikes.reshape(STEPS * blocks, width)
    history = history.reshape(-1, width)
    span = groups * blocks + 8
    dma = pltpu.SemaphoreType.DMA

    def shape(rows):
        return jax.ShapeDtypeStruct((rows, width), jnp.float32)

    def params_of(limit):
        return pltpu.CompilerParams(vmem_limit_bytes=limit * MIB)

    def cost(us):
        return pl.CostEstimate(flops=us * 10**9, bytes_accessed=us * 3 * 10**6, transcendentals=0)

    tiles = inter_weight.shape[2]
    own, *messages = pl.pallas_call(
        functools.partial(first_kernel, blocks, groups, areas),
        out_shape=(shape(groups * 3 * blocks),) + (shape(SPAN),) * 2 + (shape(2 * SPAN),) * 3,
        in_specs=[ANY] * 9,
        out_specs=(ANY,) * 6,
        scratch_shapes=[
            pltpu.SMEM((1, 1, 1, tiles), jnp.int32),
            pltpu.SMEM((1, 1, tiles), jnp.int32),
            pltpu.SMEM((1, 1, tiles), jnp.int32),
            pltpu.SMEM((1, 1, tiles), jnp.int32),
            pltpu.VMEM(spikes.shape, jnp.int32),
            pltpu.VMEM((8, width), jnp.float32),
            pltpu.VMEM((8, width), jnp.float32),
            pltpu.VMEM(history.shape, jnp.int32),
            pltpu.VMEM((tiles, width, width), jnp.float32),
            pltpu.VMEM((areas * SPAN, width), jnp.float32),
            pltpu.VMEM((3 * blocks, width), jnp.float32),
            dma((8,)),
            dma((tiles // CHUNK,)),
            dma((groups,)),
            dma((5,)),
            pltpu.SMEM((tiles,), jnp.int32),
            pltpu.SMEM((areas,), jnp.int32),
        ],
        compiler_params=params_of(LIMITS[0]),
        cost_estimate=cost(3),
        name="first",
    )(
        jnp.swapaxes(inter_area, 2, 3),
        inter_source,
        inter_block,
        inter_delay,
        spikes,
        synapse_decay,
        membrane_rate,
        history,
        inter_weight,
    )
    params = exchange(own, "grp", groups)

    def swapped(rows):
        return lax.ppermute(rows, "area", [(i, i ^ 1) for i in range(areas)])

    got = [
        lax.ppermute(messages[j + 1], "area", [(i, i ^ (2 * j)) for i in range(areas)]) for j in (2, 1, 3)
    ]
    arrived = [messages[0], swapped(messages[1])]

    tiles = intra_weight.shape[2]
    zeros = pl.pallas_call(
        clear_kernel,
        out_shape=shape(8),
        out_specs=VMEM,
        compiler_params=params_of(2),
        cost_estimate=cost(6),
        name="clear",
    )()
    intra = pl.pallas_call(
        functools.partial(intra_kernel, blocks),
        out_shape=shape(STEPS * tiles + 8),
        in_specs=[SMEM] + [VMEM] * 3,
        out_specs=VMEM,
        compiler_params=params_of(LIMITS[1]),
        cost_estimate=cost(4),
        name="intra",
    )(intra_source, zeros, spikes, intra_weight)
    *got, intra = lax.optimization_barrier((*got, intra))
    for rows in got:
        arrived += [rows, swapped(rows[SPAN:])]

    message = pl.pallas_call(
        functools.partial(merge_kernel, blocks, groups, areas, span),
        out_shape=shape(groups * 2 * blocks),
        in_specs=[SMEM, VMEM, VMEM] + [VMEM] * areas,
        out_specs=VMEM,
        scratch_shapes=[
            pltpu.VMEM((STEPS * span, width), jnp.float32),
            pltpu.SMEM((areas, 128), jnp.float32),
            dma((areas,)),
        ],
        compiler_params=params_of(LIMITS[2]),
        cost_estimate=cost(2),
        name="merge",
    )(intra_target, params, intra, *arrived)
    sums = exchange(message, "grp", groups)

    return pl.pallas_call(
        functools.partial(finish_kernel, blocks, groups),
        out_shape=(jax.ShapeDtypeStruct(voltage_init.shape, jnp.float32),) * 2,
        in_specs=[VMEM] * 6,
        out_specs=(VMEM, VMEM),
        compiler_params=params_of(LIMITS[2]),
        cost_estimate=cost(1),
        name="finish",
    )(sums, spikes, voltage_init, synapse_init, membrane_rate, synapse_decay)


def solution(mesh):
    in_specs = (
        P(None, "area", "grp", None),
        P(None, "area", "grp", None),
        P("area", "grp", None),
        P("area", "grp", None),
        P("area", "grp", None, None, None),
        P("area", "grp", None, None),
        P("area", "grp", None),
        P("area", "grp", None),
        P("area", "grp", None),
        P("area", "grp", None, None, None),
        P("area", "grp", None),
        P("area", "grp", None),
        P("area", "grp", None),
        P("area", "grp", None),
    )
    out_specs = (P("area", "grp", None), P("area", "grp", None))
    return jax.shard_map(shards, mesh=mesh, in_specs=in_specs, out_specs=out_specs, check_vma=False)
```

```python
import functools

import jax
import jax.numpy as jnp
from jax import lax
from jax.experimental import pallas as pl
from jax.experimental.pallas import tpu as pltpu
from jax.sharding import PartitionSpec as P

RESET_LEVEL = -1.0
STEPS = 10
ROOM = 12
SPAN = 128
CHUNK = 16
GROUP = 4
LIMITS = (60, 4, 8)
MIB = 1 << 20

SMEM = pl.BlockSpec(memory_space=pltpu.SMEM)
VMEM = pl.BlockSpec(memory_space=pltpu.VMEM)
ANY = pl.BlockSpec(memory_space=pl.ANY)


def started(copies):
    copies = list(copies)
    for copy in copies:
        copy.start()
    return copies


def product(rows, weight):
    high = weight.astype(jnp.bfloat16)
    low = (weight - high.astype(jnp.float32)).astype(jnp.bfloat16)
    rows = rows.astype(jnp.float32).astype(jnp.bfloat16)
    both = jnp.concatenate([high, low], axis=0)
    return jnp.dot(jnp.concatenate([rows, rows], axis=1), both, preferred_element_type=jnp.float32)


def first_kernel(blocks, groups, areas, *refs):
    inputs, own, messages, rest = refs[:9], refs[9], refs[10:15], refs[15:]
    area, source, block, delay, spikes, decay, rate, history, weight = rest[:9]
    out, tile, sems, weight_sems, own_sems, out_sems, count = rest[9:]
    rows = 3 * blocks
    targets = (
        area,
        source,
        block,
        delay,
        spikes,
        tile.at[pl.ds(0, blocks)],
        tile.at[pl.ds(blocks, blocks)],
        history,
    )
    copies = started(
        pltpu.make_async_copy(inputs[i].at[0] if i in (5, 6) else inputs[i], target, sems.at[i])
        for i, target in enumerate(targets)
    )
    tiles = weight.shape[0]
    weight_copies = started(
        pltpu.make_async_copy(
            inputs[8].at[0, 0, pl.ds(c * CHUNK, CHUNK)], weight.at[pl.ds(c * CHUNK, CHUNK)], weight_sems.at[c]
        )
        for c in range(tiles // CHUNK)
    )
    out[...] = jnp.zeros_like(out)
    for a in range(areas):
        count[a] = 0
    for copy in copies[4:7]:
        copy.wait()
    last = jnp.full((blocks, 128), -1.0, jnp.float32)
    for t in range(STEPS):
        last = jnp.where(spikes[pl.ds(t * blocks, blocks), :] == 1, float(t), last)
    tile[pl.ds(2 * blocks, blocks), :] = last
    own_copies = started(
        pltpu.make_async_copy(tile, own.at[pl.ds(h * rows, rows)], own_sems.at[h]) for h in range(groups)
    )
    for copy in copies[:4]:
        copy.wait()
    me = lax.axis_index("area")
    row = lax.broadcasted_iota(jnp.int32, (areas, 128), 0)
    lane = lax.broadcasted_iota(jnp.int32, (areas, 128), 1)
    names = jnp.full((areas, 128), -1, jnp.int32)
    copies[7].wait()
    for k in range(tiles):
        if k % CHUNK == 0:
            weight_copies[k // CHUNK].wait()
        a = area[0, 0, 0, k] ^ me
        a = (a & 1) * 4 + (a >> 1)
        rank = count[a]
        count[a] = rank + 1
        names = jnp.where((row == a) & (lane == rank), block[0, 0, k], names)
        first = (STEPS - 1 - delay[0, 0, k]) * blocks + source[0, 0, k]
        picked = history[pl.ds(first, STEPS, stride=blocks), :]
        out[pl.ds(a * SPAN + rank, STEPS, stride=ROOM), :] = product(picked, weight[k])
    names = names.astype(jnp.float32)
    for a in range(areas):
        out[pl.ds(a * SPAN + STEPS * ROOM, 1), :] = names[a : a + 1, :]
    out_copies = started(
        pltpu.make_async_copy(out.at[pl.ds(j * SPAN, n * SPAN)], message.at[pl.ds(0, n * SPAN)], out_sems.at[j])
        for j, (n, message) in enumerate(zip((1, 1, 1, 1, 4), messages))
    )
    for copy in own_copies + out_copies:
        copy.wait()


def pack_kernel(across, *refs):
    outs, sems = refs[3:6], refs[6]
    for copy in started(
        pltpu.make_async_copy(across.at[pl.ds((j + 1) * SPAN, SPAN)], out.at[pl.ds(SPAN, SPAN)], sems.at[j])
        for j, out in enumerate(outs)
    ):
        copy.wait()


def intra_kernel(blocks, source, spikes, weight, out):
    tiles = weight.shape[2]
    for k in range(tiles):
        rows = spikes[pl.ds(source[0, 0, k], STEPS, stride=blocks), :]
        out[pl.ds(k, STEPS, stride=tiles), :] = product(rows, weight[0, 0, k])


def contracted(blocks, span, total, params, h):
    base = h * 3 * blocks
    decay = params[pl.ds(base, blocks), :]
    rate = params[pl.ds(base + blocks, blocks), :]
    last = params[pl.ds(base + 2 * blocks, blocks), :]
    synapse = jnp.zeros((blocks, 128), jnp.float32)
    voltage = synapse
    for t in range(STEPS):
        synapse = decay * synapse + total[pl.ds(t * span + h * blocks, blocks), :]
        voltage = voltage + rate * (synapse - voltage)
        voltage = jnp.where(last == float(t), 0.0, voltage)
    return synapse, voltage


def add_rows(total, span, blocks_of, rows_of):
    spots = [pl.ds(b, STEPS, stride=span) for b in blocks_of]
    sums = [total[spot, :] for spot in spots]
    for i, rows in enumerate(rows_of):
        before = sums[i]
        for j in range(i):
            before = jnp.where(blocks_of[i] == blocks_of[j], sums[j], before)
        sums[i] = before + rows
    for spot, value in zip(spots, sums):
        total[spot, :] = value


def merge_kernel(blocks, groups, areas, span, target, params, intra, mine, across, *refs):
    arrived = [(mine, 0), (across, 0)] + [(refs[j], e * SPAN) for j in range(3) for e in range(2)]
    out, total, names, sems = refs[3:]
    copies = started(
        pltpu.make_async_copy(ref.at[pl.ds(first + STEPS * ROOM, 1)], names.at[pl.ds(a, 1)], sems.at[a])
        for a, (ref, first) in enumerate(arrived)
    )
    total[...] = jnp.zeros_like(total)
    tiles = target.shape[2]
    for k in range(0, tiles, GROUP):
        group = range(k, k + GROUP)
        add_rows(
            total,
            span,
            [target[0, 0, i] for i in group],
            [intra[pl.ds(i, STEPS, stride=tiles), :] for i in group],
        )
    for copy in copies:
        copy.wait()
    for a, (ref, first) in enumerate(arrived):
        for r in range(0, ROOM, GROUP):
            group = range(r, r + GROUP)
            found = [names[a, i].astype(jnp.int32) for i in group]
            add_rows(
                total,
                span,
                [jnp.where(b < 0, groups * blocks, b) for b in found],
                [ref[pl.ds(first + i, STEPS, stride=ROOM), :] for i in group],
            )

    def body(h, _):
        synapse, voltage = contracted(blocks, span, total, params, h)
        out[pl.ds(h * 2 * blocks, blocks), :] = synapse
        out[pl.ds(h * 2 * blocks + blocks, blocks), :] = voltage
        return 0

    lax.fori_loop(0, groups, body, 0, unroll=4)


def finish_kernel(blocks, groups, arrived, spikes, voltage_in, synapse_in, rate_in, decay_in, voltage_out, synapse_out):
    voltage, synapse, rate, decay = voltage_in[0], synapse_in[0], rate_in[0], decay_in[0]
    for t in range(STEPS):
        synapse = decay * synapse
        voltage = voltage + rate * (synapse - voltage)
        voltage = jnp.where(spikes[pl.ds(t * blocks, blocks), :] == 1, RESET_LEVEL, voltage)
    synapse_sum = arrived[pl.ds(0, blocks), :]
    voltage_sum = arrived[pl.ds(blocks, blocks), :]
    for h in range(1, groups):
        synapse_sum += arrived[pl.ds(h * 2 * blocks, blocks), :]
        voltage_sum += arrived[pl.ds(h * 2 * blocks + blocks, blocks), :]
    voltage_out[0] = voltage + voltage_sum
    synapse_out[0] = synapse + synapse_sum


def exchange(rows, axis, parts):
    width = rows.shape[1]
    rows = rows.reshape(parts, -1, width)
    return lax.all_to_all(rows, axis, split_axis=0, concat_axis=0, tiled=True).reshape(-1, width)


def shards(
    spikes,
    history,
    intra_source,
    intra_target,
    intra_weight,
    inter_area,
    inter_source,
    inter_block,
    inter_delay,
    inter_weight,
    voltage_init,
    synapse_init,
    membrane_rate,
    synapse_decay,
):
    blocks, width = spikes.shape[2:]
    groups, areas = lax.axis_size("grp"), lax.axis_size("area")
    spikes = spikes.reshape(STEPS * blocks, width)
    history = history.reshape(-1, width)
    span = groups * blocks + 8
    dma = pltpu.SemaphoreType.DMA

    def shape(rows):
        return jax.ShapeDtypeStruct((rows, width), jnp.float32)

    def params_of(limit):
        return pltpu.CompilerParams(vmem_limit_bytes=limit * MIB)

    def cost(us):
        return pl.CostEstimate(flops=us * 10**9, bytes_accessed=us * 3 * 10**6, transcendentals=0)

    tiles = inter_weight.shape[2]
    own, mine, *along, across = pl.pallas_call(
        functools.partial(first_kernel, blocks, groups, areas),
        out_shape=(shape(groups * 3 * blocks), shape(SPAN)) + (shape(2 * SPAN),) * 3 + (shape(4 * SPAN),),
        in_specs=[ANY] * 9,
        out_specs=(ANY,) * 6,
        scratch_shapes=[
            pltpu.SMEM((1, 1, 1, tiles), jnp.int32),
            pltpu.SMEM((1, 1, tiles), jnp.int32),
            pltpu.SMEM((1, 1, tiles), jnp.int32),
            pltpu.SMEM((1, 1, tiles), jnp.int32),
            pltpu.VMEM(spikes.shape, jnp.int32),
            pltpu.VMEM((8, width), jnp.float32),
            pltpu.VMEM((8, width), jnp.float32),
            pltpu.VMEM(history.shape, jnp.int32),
            pltpu.VMEM((tiles, width, width), jnp.float32),
            pltpu.VMEM((areas * SPAN, width), jnp.float32),
            pltpu.VMEM((3 * blocks, width), jnp.float32),
            dma((8,)),
            dma((tiles // CHUNK,)),
            dma((groups,)),
            dma((5,)),
            pltpu.SMEM((areas,), jnp.int32),
        ],
        compiler_params=params_of(LIMITS[0]),
        cost_estimate=cost(3),
        name="first",
    )(
        jnp.swapaxes(inter_area, 2, 3),
        inter_source,
        inter_block,
        inter_delay,
        spikes,
        synapse_decay,
        membrane_rate,
        history,
        inter_weight,
    )
    params = exchange(own, "grp", groups)

    across = lax.ppermute(across, "area", [(i, i ^ 1) for i in range(areas)])
    packed = pl.pallas_call(
        pack_kernel,
        out_shape=(shape(2 * SPAN),) * 3,
        in_specs=[ANY] * 4,
        out_specs=(ANY,) * 3,
        input_output_aliases={1: 0, 2: 1, 3: 2},
        scratch_shapes=[dma((3,))],
        compiler_params=params_of(2),
        cost_estimate=cost(6),
        name="pack",
    )(across, *along)
    got = [lax.ppermute(packed[j - 1], "area", [(i, i ^ (2 * j)) for i in range(areas)]) for j in (2, 1, 3)]

    intra = pl.pallas_call(
        functools.partial(intra_kernel, blocks),
        out_shape=shape(STEPS * intra_weight.shape[2]),
        in_specs=[SMEM] + [VMEM] * 2,
        out_specs=VMEM,
        compiler_params=params_of(LIMITS[1]),
        cost_estimate=cost(4),
        name="intra",
    )(intra_source, spikes, intra_weight)
    *got, intra = lax.optimization_barrier((*got, intra))

    message = pl.pallas_call(
        functools.partial(merge_kernel, blocks, groups, areas, span),
        out_shape=shape(groups * 2 * blocks),
        in_specs=[SMEM] + [VMEM] * 7,
        out_specs=VMEM,
        scratch_shapes=[
            pltpu.VMEM((STEPS * span, width), jnp.float32),
            pltpu.SMEM((areas, 128), jnp.float32),
            dma((areas,)),
        ],
        compiler_params=params_of(LIMITS[2]),
        cost_estimate=cost(2),
        name="merge",
    )(intra_target, params, intra, mine, across, *got)
    sums = exchange(message, "grp", groups)

    return pl.pallas_call(
        functools.partial(finish_kernel, blocks, groups),
        out_shape=(jax.ShapeDtypeStruct(voltage_init.shape, jnp.float32),) * 2,
        in_specs=[VMEM] * 6,
        out_specs=(VMEM, VMEM),
        compiler_params=params_of(LIMITS[2]),
        cost_estimate=cost(1),
        name="finish",
    )(sums, spikes, voltage_init, synapse_init, membrane_rate, synapse_decay)


def solution(mesh):
    in_specs = (
        P(None, "area", "grp", None),
        P(None, "area", "grp", None),
        P("area", "grp", None),
        P("area", "grp", None),
        P("area", "grp", None, None, None),
        P("area", "grp", None, None),
        P("area", "grp", None),
        P("area", "grp", None),
        P("area", "grp", None),
        P("area", "grp", None, None, None),
        P("area", "grp", None),
        P("area", "grp", None),
        P("area", "grp", None),
        P("area", "grp", None),
    )
    out_specs = (P("area", "grp", None), P("area", "grp", None))
    return jax.shard_map(shards, mesh=mesh, in_specs=in_specs, out_specs=out_specs, check_vma=False)
```

```python
import functools

import jax
import jax.numpy as jnp
from jax import lax
from jax.experimental import pallas as pl
from jax.experimental.pallas import tpu as pltpu
from jax.sharding import PartitionSpec as P

RESET_LEVEL = -1.0
STEPS = 10
ROOM = 12
SPAN = 128
CHUNK = 16
GROUP = 4
LIMITS = (60, 4, 8)
MIB = 1 << 20

SMEM = pl.BlockSpec(memory_space=pltpu.SMEM)
VMEM = pl.BlockSpec(memory_space=pltpu.VMEM)
ANY = pl.BlockSpec(memory_space=pl.ANY)


def started(copies):
    copies = list(copies)
    for copy in copies:
        copy.start()
    return copies


def product(rows, weight):
    high = weight.astype(jnp.bfloat16)
    low = (weight - high.astype(jnp.float32)).astype(jnp.bfloat16)
    rows = rows.astype(jnp.float32).astype(jnp.bfloat16)
    both = jnp.concatenate([high, low], axis=0)
    return jnp.dot(jnp.concatenate([rows, rows], axis=1), both, preferred_element_type=jnp.float32)


def first_kernel(blocks, groups, areas, *refs):
    inputs, own, messages, rest = refs[:9], refs[9], refs[10:15], refs[15:]
    area, source, block, delay, spikes, decay, rate, history, weight = rest[:9]
    out, tile, sems, weight_sems, own_sems, out_sems = rest[9:]
    rows = 3 * blocks
    targets = (
        area,
        source,
        block,
        delay,
        spikes,
        tile.at[pl.ds(0, blocks)],
        tile.at[pl.ds(blocks, blocks)],
        history,
    )
    copies = started(
        pltpu.make_async_copy(inputs[i].at[0] if i in (5, 6) else inputs[i], target, sems.at[i])
        for i, target in enumerate(targets)
    )
    tiles = weight.shape[0]
    weight_copies = started(
        pltpu.make_async_copy(
            inputs[8].at[0, 0, pl.ds(c * CHUNK, CHUNK)], weight.at[pl.ds(c * CHUNK, CHUNK)], weight_sems.at[c]
        )
        for c in range(tiles // CHUNK)
    )
    out[...] = jnp.zeros_like(out)
    for copy in copies[4:7]:
        copy.wait()
    last = jnp.full((blocks, 128), -1.0, jnp.float32)
    for t in range(STEPS):
        last = jnp.where(spikes[pl.ds(t * blocks, blocks), :] == 1, float(t), last)
    tile[pl.ds(2 * blocks, blocks), :] = last
    own_copies = started(
        pltpu.make_async_copy(tile, own.at[pl.ds(h * rows, rows)], own_sems.at[h]) for h in range(groups)
    )
    for copy in copies[:4]:
        copy.wait()
    me = lax.axis_index("area")
    lane = lax.broadcasted_iota(jnp.int32, (areas, 128), 1)
    slot = jnp.where(lane < 16, lax.broadcasted_iota(jnp.int32, (areas, 128), 0) * 16 + lane, -1)
    names = jnp.full((areas, 128), -1, jnp.int32)
    counts = jnp.int32(0)
    copies[7].wait()
    for k in range(tiles):
        if k % CHUNK == 0:
            weight_copies[k // CHUNK].wait()
        a = area[0, 0, 0, k] ^ me
        a = (a & 1) * 4 + (a >> 1)
        rank = (counts >> (a * 4)) & 15
        counts = counts + (jnp.int32(1) << (a * 4))
        names = jnp.where(slot == a * 16 + rank, block[0, 0, k], names)
        first = (STEPS - 1 - delay[0, 0, k]) * blocks + source[0, 0, k]
        picked = history[pl.ds(first, STEPS, stride=blocks), :]
        out[pl.ds(a * SPAN + rank, STEPS, stride=ROOM), :] = product(picked, weight[k])
    names = names.astype(jnp.float32)
    for a in range(areas):
        out[pl.ds(a * SPAN + STEPS * ROOM, 1), :] = names[a : a + 1, :]
    out_copies = started(
        pltpu.make_async_copy(out.at[pl.ds(j * SPAN, n * SPAN)], message.at[pl.ds(0, n * SPAN)], out_sems.at[j])
        for j, (n, message) in enumerate(zip((1, 1, 1, 1, 4), messages))
    )
    for copy in own_copies + out_copies:
        copy.wait()


def pack_kernel(across, *refs):
    outs, sems = refs[3:6], refs[6]
    for copy in started(
        pltpu.make_async_copy(across.at[pl.ds((j + 1) * SPAN, SPAN)], out.at[pl.ds(SPAN, SPAN)], sems.at[j])
        for j, out in enumerate(outs)
    ):
        copy.wait()


def intra_kernel(blocks, source, spikes, weight, out):
    tiles = weight.shape[2]
    for k in range(tiles):
        rows = spikes[pl.ds(source[0, 0, k], STEPS, stride=blocks), :]
        out[pl.ds(k, STEPS, stride=tiles), :] = product(rows, weight[0, 0, k])


def contracted(blocks, span, total, params, h):
    base = h * 3 * blocks
    decay = params[pl.ds(base, blocks), :]
    rate = params[pl.ds(base + blocks, blocks), :]
    last = params[pl.ds(base + 2 * blocks, blocks), :]
    synapse = jnp.zeros((blocks, 128), jnp.float32)
    voltage = synapse
    for t in range(STEPS):
        synapse = decay * synapse + total[pl.ds(t * span + h * blocks, blocks), :]
        voltage = voltage + rate * (synapse - voltage)
        voltage = jnp.where(last == float(t), 0.0, voltage)
    return synapse, voltage


def add_rows(total, span, blocks_of, rows_of):
    spots = [pl.ds(b, STEPS, stride=span) for b in blocks_of]
    sums = [total[spot, :] for spot in spots]
    for i, rows in enumerate(rows_of):
        before = sums[i]
        for j in range(i):
            before = jnp.where(blocks_of[i] == blocks_of[j], sums[j], before)
        sums[i] = before + rows
    for spot, value in zip(spots, sums):
        total[spot, :] = value


def merge_kernel(blocks, groups, areas, span, target, params, intra, mine, across, *refs):
    arrived = [(mine, 0), (across, 0)] + [(refs[j], e * SPAN) for j in range(3) for e in range(2)]
    out, total, names, sems = refs[3:]
    copies = started(
        pltpu.make_async_copy(ref.at[pl.ds(first + STEPS * ROOM, 1)], names.at[pl.ds(a, 1)], sems.at[a])
        for a, (ref, first) in enumerate(arrived)
    )
    total[...] = jnp.zeros_like(total)
    tiles = target.shape[2]
    for k in range(0, tiles, GROUP):
        group = range(k, k + GROUP)
        add_rows(
            total,
            span,
            [target[0, 0, i] for i in group],
            [intra[pl.ds(i, STEPS, stride=tiles), :] for i in group],
        )
    for copy in copies:
        copy.wait()
    for a, (ref, first) in enumerate(arrived):
        for r in range(0, ROOM, GROUP):
            group = range(r, r + GROUP)
            found = [names[a, i].astype(jnp.int32) for i in group]
            add_rows(
                total,
                span,
                [jnp.where(b < 0, groups * blocks, b) for b in found],
                [ref[pl.ds(first + i, STEPS, stride=ROOM), :] for i in group],
            )

    def body(h, _):
        synapse, voltage = contracted(blocks, span, total, params, h)
        out[pl.ds(h * 2 * blocks, blocks), :] = synapse
        out[pl.ds(h * 2 * blocks + blocks, blocks), :] = voltage
        return 0

    lax.fori_loop(0, groups, body, 0, unroll=16)


def finish_kernel(blocks, groups, arrived, spikes, voltage_in, synapse_in, rate_in, decay_in, voltage_out, synapse_out):
    voltage, synapse, rate, decay = voltage_in[0], synapse_in[0], rate_in[0], decay_in[0]
    for t in range(STEPS):
        synapse = decay * synapse
        voltage = voltage + rate * (synapse - voltage)
        voltage = jnp.where(spikes[pl.ds(t * blocks, blocks), :] == 1, RESET_LEVEL, voltage)
    synapse_sum = arrived[pl.ds(0, blocks), :]
    voltage_sum = arrived[pl.ds(blocks, blocks), :]
    for h in range(1, groups):
        synapse_sum += arrived[pl.ds(h * 2 * blocks, blocks), :]
        voltage_sum += arrived[pl.ds(h * 2 * blocks + blocks, blocks), :]
    voltage_out[0] = voltage + voltage_sum
    synapse_out[0] = synapse + synapse_sum


def exchange(rows, axis, parts):
    width = rows.shape[1]
    rows = rows.reshape(parts, -1, width)
    return lax.all_to_all(rows, axis, split_axis=0, concat_axis=0, tiled=True).reshape(-1, width)


def shards(
    spikes,
    history,
    intra_source,
    intra_target,
    intra_weight,
    inter_area,
    inter_source,
    inter_block,
    inter_delay,
    inter_weight,
    voltage_init,
    synapse_init,
    membrane_rate,
    synapse_decay,
):
    blocks, width = spikes.shape[2:]
    groups, areas = lax.axis_size("grp"), lax.axis_size("area")
    spikes = spikes.reshape(STEPS * blocks, width)
    history = history.reshape(-1, width)
    span = groups * blocks + 8
    dma = pltpu.SemaphoreType.DMA

    def shape(rows):
        return jax.ShapeDtypeStruct((rows, width), jnp.float32)

    def params_of(limit):
        return pltpu.CompilerParams(vmem_limit_bytes=limit * MIB)

    def cost(us):
        return pl.CostEstimate(flops=us * 10**9, bytes_accessed=us * 3 * 10**6, transcendentals=0)

    tiles = inter_weight.shape[2]
    own, mine, *along, across = pl.pallas_call(
        functools.partial(first_kernel, blocks, groups, areas),
        out_shape=(shape(groups * 3 * blocks), shape(SPAN)) + (shape(2 * SPAN),) * 3 + (shape(4 * SPAN),),
        in_specs=[ANY] * 9,
        out_specs=(ANY,) * 6,
        scratch_shapes=[
            pltpu.SMEM((1, 1, 1, tiles), jnp.int32),
            pltpu.SMEM((1, 1, tiles), jnp.int32),
            pltpu.SMEM((1, 1, tiles), jnp.int32),
            pltpu.SMEM((1, 1, tiles), jnp.int32),
            pltpu.VMEM(spikes.shape, jnp.int32),
            pltpu.VMEM((8, width), jnp.float32),
            pltpu.VMEM((8, width), jnp.float32),
            pltpu.VMEM(history.shape, jnp.int32),
            pltpu.VMEM((tiles, width, width), jnp.float32),
            pltpu.VMEM((areas * SPAN, width), jnp.float32),
            pltpu.VMEM((3 * blocks, width), jnp.float32),
            dma((8,)),
            dma((tiles // CHUNK,)),
            dma((groups,)),
            dma((5,)),
        ],
        compiler_params=params_of(LIMITS[0]),
        cost_estimate=cost(3),
        name="first",
    )(
        jnp.swapaxes(inter_area, 2, 3),
        inter_source,
        inter_block,
        inter_delay,
        spikes,
        synapse_decay,
        membrane_rate,
        history,
        inter_weight,
    )
    params = exchange(own, "grp", groups)

    across = lax.ppermute(across, "area", [(i, i ^ 1) for i in range(areas)])
    packed = pl.pallas_call(
        pack_kernel,
        out_shape=(shape(2 * SPAN),) * 3,
        in_specs=[ANY] * 4,
        out_specs=(ANY,) * 3,
        input_output_aliases={1: 0, 2: 1, 3: 2},
        scratch_shapes=[dma((3,))],
        compiler_params=params_of(2),
        cost_estimate=cost(6),
        name="pack",
    )(across, *along)
    got = [lax.ppermute(packed[j - 1], "area", [(i, i ^ (2 * j)) for i in range(areas)]) for j in (1, 3, 2)]

    intra = pl.pallas_call(
        functools.partial(intra_kernel, blocks),
        out_shape=shape(STEPS * intra_weight.shape[2]),
        in_specs=[SMEM] + [VMEM] * 2,
        out_specs=VMEM,
        compiler_params=params_of(LIMITS[1]),
        cost_estimate=cost(4),
        name="intra",
    )(intra_source, spikes, intra_weight)
    *got, intra = lax.optimization_barrier((*got, intra))

    message = pl.pallas_call(
        functools.partial(merge_kernel, blocks, groups, areas, span),
        out_shape=shape(groups * 2 * blocks),
        in_specs=[SMEM] + [VMEM] * 7,
        out_specs=VMEM,
        scratch_shapes=[
            pltpu.VMEM((STEPS * span, width), jnp.float32),
            pltpu.SMEM((areas, 128), jnp.float32),
            dma((areas,)),
        ],
        compiler_params=params_of(LIMITS[2]),
        cost_estimate=cost(2),
        name="merge",
    )(intra_target, params, intra, mine, across, *got)
    sums = exchange(message, "grp", groups)

    return pl.pallas_call(
        functools.partial(finish_kernel, blocks, groups),
        out_shape=(jax.ShapeDtypeStruct(voltage_init.shape, jnp.float32),) * 2,
        in_specs=[VMEM] * 6,
        out_specs=(VMEM, VMEM),
        compiler_params=params_of(LIMITS[2]),
        cost_estimate=cost(1),
        name="finish",
    )(sums, spikes, voltage_init, synapse_init, membrane_rate, synapse_decay)


def solution(mesh):
    in_specs = (
        P(None, "area", "grp", None),
        P(None, "area", "grp", None),
        P("area", "grp", None),
        P("area", "grp", None),
        P("area", "grp", None, None, None),
        P("area", "grp", None, None),
        P("area", "grp", None),
        P("area", "grp", None),
        P("area", "grp", None),
        P("area", "grp", None, None, None),
        P("area", "grp", None),
        P("area", "grp", None),
        P("area", "grp", None),
        P("area", "grp", None),
    )
    out_specs = (P("area", "grp", None), P("area", "grp", None))
    return jax.shard_map(shards, mesh=mesh, in_specs=in_specs, out_specs=out_specs, check_vma=False)
```

```python
import functools

import jax
import jax.numpy as jnp
from jax import lax
from jax.experimental import pallas as pl
from jax.experimental.pallas import tpu as pltpu
from jax.sharding import PartitionSpec as P

RESET_LEVEL = -1.0
STEPS = 10
ROOM = 12
SPAN = 128
CHUNK = 16
GROUP = 4
LIMITS = (60, 4, 8)
MIB = 1 << 20

SMEM = pl.BlockSpec(memory_space=pltpu.SMEM)
VMEM = pl.BlockSpec(memory_space=pltpu.VMEM)
ANY = pl.BlockSpec(memory_space=pl.ANY)


def started(copies):
    copies = list(copies)
    for copy in copies:
        copy.start()
    return copies


def product(rows, weight):
    high = weight.astype(jnp.bfloat16)
    low = (weight - high.astype(jnp.float32)).astype(jnp.bfloat16)
    rows = rows.astype(jnp.float32).astype(jnp.bfloat16)
    both = jnp.concatenate([high, low], axis=0)
    return jnp.dot(jnp.concatenate([rows, rows], axis=1), both, preferred_element_type=jnp.float32)


def first_kernel(blocks, groups, areas, *refs):
    inputs, own, messages, rest = refs[:9], refs[9], refs[10:15], refs[15:]
    area, source, block, delay, spikes, decay, rate, history, weight = rest[:9]
    out, tile, sems, weight_sems, own_sems, out_sems = rest[9:]
    rows = 3 * blocks
    targets = (
        area,
        source,
        block,
        delay,
        spikes,
        tile.at[pl.ds(0, blocks)],
        tile.at[pl.ds(blocks, blocks)],
        history,
    )
    copies = started(
        pltpu.make_async_copy(inputs[i].at[0] if i in (5, 6) else inputs[i], target, sems.at[i])
        for i, target in enumerate(targets)
    )
    tiles = weight.shape[0]
    weight_copies = started(
        pltpu.make_async_copy(
            inputs[8].at[0, 0, pl.ds(c * CHUNK, CHUNK)], weight.at[pl.ds(c * CHUNK, CHUNK)], weight_sems.at[c]
        )
        for c in range(tiles // CHUNK)
    )
    out[...] = jnp.zeros_like(out)
    for copy in copies[4:7]:
        copy.wait()
    last = jnp.full((blocks, 128), -1.0, jnp.float32)
    for t in range(STEPS):
        last = jnp.where(spikes[pl.ds(t * blocks, blocks), :] == 1, float(t), last)
    tile[pl.ds(2 * blocks, blocks), :] = last
    own_copies = started(
        pltpu.make_async_copy(tile, own.at[pl.ds(h * rows, rows)], own_sems.at[h]) for h in range(groups)
    )
    for copy in copies[:4]:
        copy.wait()
    me = lax.axis_index("area")
    lane = lax.broadcasted_iota(jnp.int32, (areas, 128), 1)
    slot = jnp.where(lane < 16, lax.broadcasted_iota(jnp.int32, (areas, 128), 0) * 16 + lane, -1)
    names = jnp.full((areas, 128), -1, jnp.int32)
    counts = jnp.int32(0)
    copies[7].wait()
    for k in range(tiles):
        if k % CHUNK == 0:
            weight_copies[k // CHUNK].wait()
        a = area[0, 0, 0, k] ^ me
        a = (a & 1) * 4 + (a >> 1)
        rank = (counts >> (a * 4)) & 15
        counts = counts + (jnp.int32(1) << (a * 4))
        names = jnp.where(slot == a * 16 + rank, block[0, 0, k], names)
        first = (STEPS - 1 - delay[0, 0, k]) * blocks + source[0, 0, k]
        picked = history[pl.ds(first, STEPS, stride=blocks), :]
        out[pl.ds(a * SPAN + rank, STEPS, stride=ROOM), :] = product(picked, weight[k])
    names = names.astype(jnp.float32)
    for a in range(areas):
        out[pl.ds(a * SPAN + STEPS * ROOM, 1), :] = names[a : a + 1, :]
    out_copies = started(
        pltpu.make_async_copy(out.at[pl.ds(j * SPAN, n * SPAN)], message.at[pl.ds(0, n * SPAN)], out_sems.at[j])
        for j, (n, message) in enumerate(zip((1, 1, 1, 1, 4), messages))
    )
    for copy in own_copies + out_copies:
        copy.wait()


def pack_kernel(across, *refs):
    outs, sems = refs[3:6], refs[6]
    for copy in started(
        pltpu.make_async_copy(across.at[pl.ds((j + 1) * SPAN, SPAN)], out.at[pl.ds(SPAN, SPAN)], sems.at[j])
        for j, out in enumerate(outs)
    ):
        copy.wait()


def intra_kernel(blocks, source, spikes, weight, out):
    tiles = weight.shape[2]
    for k in range(tiles):
        rows = spikes[pl.ds(source[0, 0, k], STEPS, stride=blocks), :]
        out[pl.ds(k, STEPS, stride=tiles), :] = product(rows, weight[0, 0, k])


def contracted(blocks, span, total, params, h):
    base = h * 3 * blocks
    decay = params[pl.ds(base, blocks), :]
    rate = params[pl.ds(base + blocks, blocks), :]
    last = params[pl.ds(base + 2 * blocks, blocks), :]
    synapse = jnp.zeros((blocks, 128), jnp.float32)
    voltage = synapse
    for t in range(STEPS):
        synapse = decay * synapse + total[pl.ds(t * span + h * blocks, blocks), :]
        voltage = voltage + rate * (synapse - voltage)
        voltage = jnp.where(last == float(t), 0.0, voltage)
    return synapse, voltage


def add_rows(total, span, blocks_of, rows_of):
    spots = [pl.ds(b, STEPS, stride=span) for b in blocks_of]
    sums = [total[spot, :] for spot in spots]
    for i, rows in enumerate(rows_of):
        before = sums[i]
        for j in range(i):
            before = jnp.where(blocks_of[i] == blocks_of[j], sums[j], before)
        sums[i] = before + rows
    for spot, value in zip(spots, sums):
        total[spot, :] = value


def merge_kernel(blocks, groups, areas, span, target, params, intra, mine, across, *refs):
    arrived = [(mine, 0), (across, 0)] + [(refs[j], e * SPAN) for j in range(3) for e in range(2)]
    out, total, names, sems = refs[3:]
    copies = started(
        pltpu.make_async_copy(ref.at[pl.ds(first + STEPS * ROOM, 1)], names.at[pl.ds(a, 1)], sems.at[a])
        for a, (ref, first) in enumerate(arrived)
    )
    total[...] = jnp.zeros_like(total)
    tiles = target.shape[2]
    for k in range(0, tiles, GROUP):
        group = range(k, k + GROUP)
        add_rows(
            total,
            span,
            [target[0, 0, i] for i in group],
            [intra[pl.ds(i, STEPS, stride=tiles), :] for i in group],
        )
    for copy in copies:
        copy.wait()
    for a, (ref, first) in enumerate(arrived):
        for r in range(0, ROOM, GROUP):
            group = range(r, r + GROUP)
            found = [names[a, i].astype(jnp.int32) for i in group]

            @pl.when(found[0] >= 0)
            def _(ref=ref, first=first, group=group, found=found):
                add_rows(
                    total,
                    span,
                    [jnp.where(b < 0, groups * blocks, b) for b in found],
                    [ref[pl.ds(first + i, STEPS, stride=ROOM), :] for i in group],
                )


    def body(h, _):
        synapse, voltage = contracted(blocks, span, total, params, h)
        out[pl.ds(h * 2 * blocks, blocks), :] = synapse
        out[pl.ds(h * 2 * blocks + blocks, blocks), :] = voltage
        return 0

    lax.fori_loop(0, groups, body, 0, unroll=16)


def finish_kernel(blocks, groups, arrived, spikes, voltage_in, synapse_in, rate_in, decay_in, voltage_out, synapse_out):
    voltage, synapse, rate, decay = voltage_in[0], synapse_in[0], rate_in[0], decay_in[0]
    for t in range(STEPS):
        synapse = decay * synapse
        voltage = voltage + rate * (synapse - voltage)
        voltage = jnp.where(spikes[pl.ds(t * blocks, blocks), :] == 1, RESET_LEVEL, voltage)
    synapse_sum = arrived[pl.ds(0, blocks), :]
    voltage_sum = arrived[pl.ds(blocks, blocks), :]
    for h in range(1, groups):
        synapse_sum += arrived[pl.ds(h * 2 * blocks, blocks), :]
        voltage_sum += arrived[pl.ds(h * 2 * blocks + blocks, blocks), :]
    voltage_out[0] = voltage + voltage_sum
    synapse_out[0] = synapse + synapse_sum


def exchange(rows, axis, parts):
    width = rows.shape[1]
    rows = rows.reshape(parts, -1, width)
    return lax.all_to_all(rows, axis, split_axis=0, concat_axis=0, tiled=True).reshape(-1, width)


def shards(
    spikes,
    history,
    intra_source,
    intra_target,
    intra_weight,
    inter_area,
    inter_source,
    inter_block,
    inter_delay,
    inter_weight,
    voltage_init,
    synapse_init,
    membrane_rate,
    synapse_decay,
):
    blocks, width = spikes.shape[2:]
    groups, areas = lax.axis_size("grp"), lax.axis_size("area")
    spikes = spikes.reshape(STEPS * blocks, width)
    history = history.reshape(-1, width)
    span = groups * blocks + 8
    dma = pltpu.SemaphoreType.DMA

    def shape(rows):
        return jax.ShapeDtypeStruct((rows, width), jnp.float32)

    def params_of(limit):
        return pltpu.CompilerParams(vmem_limit_bytes=limit * MIB)

    def cost(us):
        return pl.CostEstimate(flops=us * 10**9, bytes_accessed=us * 3 * 10**6, transcendentals=0)

    tiles = inter_weight.shape[2]
    own, mine, *along, across = pl.pallas_call(
        functools.partial(first_kernel, blocks, groups, areas),
        out_shape=(shape(groups * 3 * blocks), shape(SPAN)) + (shape(2 * SPAN),) * 3 + (shape(4 * SPAN),),
        in_specs=[ANY] * 9,
        out_specs=(ANY,) * 6,
        scratch_shapes=[
            pltpu.SMEM((1, 1, 1, tiles), jnp.int32),
            pltpu.SMEM((1, 1, tiles), jnp.int32),
            pltpu.SMEM((1, 1, tiles), jnp.int32),
            pltpu.SMEM((1, 1, tiles), jnp.int32),
            pltpu.VMEM(spikes.shape, jnp.int32),
            pltpu.VMEM((8, width), jnp.float32),
            pltpu.VMEM((8, width), jnp.float32),
            pltpu.VMEM(history.shape, jnp.int32),
            pltpu.VMEM((tiles, width, width), jnp.float32),
            pltpu.VMEM((areas * SPAN, width), jnp.float32),
            pltpu.VMEM((3 * blocks, width), jnp.float32),
            dma((8,)),
            dma((tiles // CHUNK,)),
            dma((groups,)),
            dma((5,)),
        ],
        compiler_params=params_of(LIMITS[0]),
        cost_estimate=cost(3),
        name="first",
    )(
        jnp.swapaxes(inter_area, 2, 3),
        inter_source,
        inter_block,
        inter_delay,
        spikes,
        synapse_decay,
        membrane_rate,
        history,
        inter_weight,
    )
    params = exchange(own, "grp", groups)

    across = lax.ppermute(across, "area", [(i, i ^ 1) for i in range(areas)])
    packed = pl.pallas_call(
        pack_kernel,
        out_shape=(shape(2 * SPAN),) * 3,
        in_specs=[ANY] * 4,
        out_specs=(ANY,) * 3,
        input_output_aliases={1: 0, 2: 1, 3: 2},
        scratch_shapes=[dma((3,))],
        compiler_params=params_of(2),
        cost_estimate=cost(6),
        name="pack",
    )(across, *along)
    got = [lax.ppermute(packed[j - 1], "area", [(i, i ^ (2 * j)) for i in range(areas)]) for j in (1, 3, 2)]

    intra = pl.pallas_call(
        functools.partial(intra_kernel, blocks),
        out_shape=shape(STEPS * intra_weight.shape[2]),
        in_specs=[SMEM] + [VMEM] * 2,
        out_specs=VMEM,
        compiler_params=params_of(LIMITS[1]),
        cost_estimate=cost(4),
        name="intra",
    )(intra_source, spikes, intra_weight)
    *got, intra = lax.optimization_barrier((*got, intra))

    message = pl.pallas_call(
        functools.partial(merge_kernel, blocks, groups, areas, span),
        out_shape=shape(groups * 2 * blocks),
        in_specs=[SMEM] + [VMEM] * 7,
        out_specs=VMEM,
        scratch_shapes=[
            pltpu.VMEM((STEPS * span, width), jnp.float32),
            pltpu.SMEM((areas, 128), jnp.float32),
            dma((areas,)),
        ],
        compiler_params=params_of(LIMITS[2]),
        cost_estimate=cost(2),
        name="merge",
    )(intra_target, params, intra, mine, across, *got)
    sums = exchange(message, "grp", groups)

    return pl.pallas_call(
        functools.partial(finish_kernel, blocks, groups),
        out_shape=(jax.ShapeDtypeStruct(voltage_init.shape, jnp.float32),) * 2,
        in_specs=[VMEM] * 6,
        out_specs=(VMEM, VMEM),
        compiler_params=params_of(LIMITS[2]),
        cost_estimate=cost(1),
        name="finish",
    )(sums, spikes, voltage_init, synapse_init, membrane_rate, synapse_decay)


def solution(mesh):
    in_specs = (
        P(None, "area", "grp", None),
        P(None, "area", "grp", None),
        P("area", "grp", None),
        P("area", "grp", None),
        P("area", "grp", None, None, None),
        P("area", "grp", None, None),
        P("area", "grp", None),
        P("area", "grp", None),
        P("area", "grp", None),
        P("area", "grp", None, None, None),
        P("area", "grp", None),
        P("area", "grp", None),
        P("area", "grp", None),
        P("area", "grp", None),
    )
    out_specs = (P("area", "grp", None), P("area", "grp", None))
    return jax.shard_map(shards, mesh=mesh, in_specs=in_specs, out_specs=out_specs, check_vma=False)
```
